128 devices in a mesh: seq: 32 (over x_lo, z, y), kvh: 4 (over x_hi, core).
Axes of the slice: x: 4 (x_hi: 2, x_lo: 2; x = x_hi * 2 + x_lo), y: 4, z: 4, core: 2. Of those that a mesh axis runs over, the one named last changes fastest.
Arguments:
- queries: bfloat16 [32, 3584], P('seq', 'kvh'), may hold values from -120 to 120
- keys: bfloat16 [2048, 512, 512], P('seq', None, 'kvh'), may hold values from -6 to 6
- values: bfloat16 [2048, 512, 512], P('seq', None, 'kvh'), may hold values from -24 to 24
- new_keys: bfloat16 [8, 4, 512], P(None, None, 'kvh'), may hold values from -6 to 6
- new_values: bfloat16 [8, 4, 512], P(None, None, 'kvh'), may hold values from -24 to 24
- cache_len: int32 [8], replicated, may hold values from 65025 to 393216, as said below
- block_request: int32 [2048], P('seq'), may hold values from 0 to 7, as said below
- block_index: int32 [2048], P('seq'), may hold values from 0 to 767, as said below
Outputs:
- attended: bfloat16 [32, 3584], P('seq', 'kvh')
The draws below stay inside these ranges and needn't reach their ends.
Inputs may be any that keep to these rules, and one draw needn't show every extreme that they name: `cache_len`: exactly one request has 768 blocks and length 393216; every other request has at least 128 blocks, and its length lies in its last block. `block_request`: request r holds ceil(cache_len[r] / 512) blocks in all, spread over the devices. The blocks of request r carry block_index 0 to ceil(cache_len[r] / 512) - 1, each once.
All inputs are finite; a program needn't handle non-finite values.
Results may differ from the reference program's by a relative error of at most 0.0028.
Values may be sent and summed in bfloat16 or wider, within the bound.
A program may use at most 64 MiB of HBM per device.

```python
import math
import jax
import jax.numpy as jnp
from jax import lax

QH = 28
KVH = 4
HD = 128
STEPS = 4
BLOCK = 512
R = 8
BLK_DEV = 64
NBLK = 2048


def block_layout(key):
    key = jax.random.fold_in(key, 11)
    first, second, third, fourth = jax.random.split(key, 4)
    big = jax.random.randint(first, (), 0, R)
    longest = 3 * NBLK // 8
    base = NBLK // (2 * R)
    extra = NBLK - longest - (R - 1) * base
    picks = jax.random.randint(second, (max(extra, 1),), 0, R - 1)
    hits = jnp.sum((picks[:, None] == jnp.arange(R - 1, dtype=jnp.int32)[None, :]).astype(jnp.int32), axis=0)
    hits = hits * (1 if extra > 0 else 0)
    others = base + hits
    ids = jnp.arange(R, dtype=jnp.int32)
    shifted = jnp.take(others, jnp.clip(ids - (ids > big).astype(jnp.int32), 0, R - 2))
    counts = jnp.where(ids == big, longest, shifted)
    ends = jnp.cumsum(counts)
    starts = ends - counts
    slots = jnp.arange(NBLK, dtype=jnp.int32)
    owner = jnp.sum((slots[:, None] >= ends[None, :]).astype(jnp.int32), axis=1)
    index = slots - jnp.take(starts, owner)
    order = jax.random.permutation(third, NBLK)
    cut = jax.random.randint(fourth, (R,), 0, BLOCK)
    cut = jnp.where(ids == big, 0, cut)
    lengths = counts * BLOCK - cut
    return (owner[order].astype(jnp.int32), index[order].astype(jnp.int32), lengths.astype(jnp.int32))


def draw_cache_len(key, part):
    return block_layout(key)[2]


def draw_block_request(key, part):
    return block_layout(key)[0]


def draw_block_index(key, part):
    return block_layout(key)[1]


def draw_queries(key, part):
    key = jax.random.fold_in(key, 5)
    first = jax.random.fold_in(key, 0)
    shape = (R * STEPS, QH * HD)
    base = jnp.clip(2.0 * jax.random.normal(first, shape, jnp.float32), -12.0, 12.0)
    return base.astype(jnp.bfloat16)


def block_levels(own_key, extent, pieces, least, largest):
    gain = 1.0
    for axis_at, parts in pieces:
        steps = jax.random.uniform(jax.random.fold_in(jax.random.fold_in(own_key, 6), axis_at), (parts,), jnp.float32, least / len(pieces), largest / len(pieces))
        gain = gain * jnp.repeat(jnp.exp(steps), extent[axis_at] // parts).reshape((-1,) + (1,) * (len(extent) - 1 - axis_at))
    return gain


def noise(key, dims, deviation, most, shards=(), held_as=jnp.bfloat16):
    array = jax.random.normal(key, dims, jnp.float32) * deviation
    if len(shards) > 0:
        array = block_levels(key, dims, shards, -0.22, 0.18) * array
    return jnp.clip(array, min=-most, max=most).astype(held_as)


def setup_inputs(seed: int = 0) -> dict:
    key_of = jax.random.split(jax.random.key(seed), 9)
    queries = draw_queries(jax.random.fold_in(key_of[8], 71), 0)
    keys = noise(key_of[1], (NBLK, BLOCK, KVH * HD), 1.0, 6.0, ((0, 32), (2, 4)))
    values = noise(key_of[2], (NBLK, BLOCK, KVH * HD), 4.0, 24.0, ((0, 32), (2, 4)))
    new_keys = noise(key_of[3], (R, STEPS, KVH * HD), 1.0, 6.0, ((2, 4),))
    new_values = noise(key_of[4], (R, STEPS, KVH * HD), 4.0, 24.0, ((2, 4),))
    cache_len = draw_cache_len(jax.random.fold_in(key_of[8], 71), 0)
    block_request = draw_block_request(jax.random.fold_in(key_of[8], 71), 0)
    block_index = draw_block_index(jax.random.fold_in(key_of[8], 71), 0)
    return {"queries": queries, "keys": keys, "values": values, "new_keys": new_keys, "new_values": new_values, "cache_len": cache_len, "block_request": block_request, "block_index": block_index}


floor_value = -1e+30

def block_terms(scores, valid):
    capped = jnp.where(valid, scores, floor_value)
    top = lax.optimization_barrier(jnp.max(capped, axis=-1))
    weights = jnp.where(valid, jnp.exp(scores - top[..., None]), 0.0).astype(jnp.bfloat16)
    total = lax.optimization_barrier(jnp.sum(weights.astype(jnp.float32), axis=-1))
    return (top, total, weights)

def reference(queries, keys, values, new_keys, new_values, cache_len, block_request, block_index):
    group = QH // KVH
    rows = STEPS * group
    scale = 1.0 / math.sqrt(HD)
    high = lax.Precision.HIGHEST
    q_all = queries.reshape(R, STEPS, KVH, group, HD).transpose(0, 2, 1, 3, 4).reshape(R, KVH, rows, HD)
    nblk = keys.shape[0]
    width = BLK_DEV
    key_groups = keys.reshape(nblk // width, width, BLOCK, KVH, HD)
    value_groups = values.reshape(nblk // width, width, BLOCK, KVH, HD)
    req_groups = block_request.reshape(nblk // width, width)
    idx_groups = block_index.reshape(nblk // width, width)
    requests = jnp.arange(R, dtype=jnp.int32)
    offsets = jnp.arange(BLOCK, dtype=jnp.int32)

    def merge_group(carry, piece):
        key_g, value_g, req_g, idx_g = piece
        q_g = jnp.take(q_all, req_g, axis=0)
        scores = jnp.einsum('bhqd,bthd->bhqt', q_g.astype(jnp.float32), key_g.astype(jnp.float32)) * scale
        positions = idx_g[:, None] * BLOCK + offsets[None, :]
        valid = (positions < jnp.take(cache_len, req_g)[:, None])[:, None, None, :]
        top, total, weights = block_terms(scores, valid)
        out = jnp.einsum('bhqt,bthd->bhqd', weights.astype(jnp.float32), value_g.astype(jnp.float32))
        onehot = req_g[None, :] == requests[:, None]
        gtop = lax.optimization_barrier(jnp.max(jnp.where(onehot[:, :, None, None], top[None], floor_value), axis=1))
        ctop, ctotal, cout = carry
        best = jnp.maximum(ctop, gtop)
        keep = jnp.exp(ctop - best)
        bscale = jnp.exp(top - jnp.take(best, req_g, axis=0))
        weight_oh = onehot.astype(jnp.float32)
        ntotal = ctotal * keep + jnp.einsum('rb,bhq->rhq', weight_oh, total * bscale, precision=high)
        nout = cout * keep[..., None] + jnp.einsum('rb,bhqd->rhqd', weight_oh, out * bscale[..., None], precision=high)
        return ((best, ntotal, nout), None)
    init = (jnp.full((R, KVH, rows), floor_value, jnp.float32), jnp.zeros((R, KVH, rows), jnp.float32), jnp.zeros((R, KVH, rows, HD), jnp.float32))
    (ctop, ctotal, cout), _ = lax.scan(merge_group, init, (key_groups, value_groups, req_groups, idx_groups))
    fresh_k = new_keys.reshape(R, STEPS, KVH, HD)
    fresh_v = new_values.reshape(R, STEPS, KVH, HD)
    scores = jnp.einsum('rhqd,rthd->rhqt', q_all.astype(jnp.float32), fresh_k.astype(jnp.float32)) * scale
    row_step = jnp.arange(rows, dtype=jnp.int32) // group
    valid = (jnp.arange(STEPS, dtype=jnp.int32)[None, :] <= row_step[:, None])[None, None]
    ntop, ntotal, nweights = block_terms(scores, valid)
    nout = jnp.einsum('rhqt,rthd->rhqd', nweights.astype(jnp.float32), fresh_v.astype(jnp.float32))
    best = jnp.maximum(ctop, ntop)
    left = jnp.exp(ctop - best)
    right = jnp.exp(ntop - best)
    total = ctotal * left + ntotal * right
    summed = cout * left[..., None] + nout * right[..., None]
    result = (summed / total[..., None]).astype(jnp.bfloat16)
    return result.reshape(R, KVH, STEPS, group, HD).transpose(0, 2, 1, 3, 4).reshape(R * STEPS, QH * HD)
```

```python
import math

import jax
import jax.numpy as jnp
from jax import lax
from jax.experimental import pallas as pl
from jax.experimental.pallas import tpu as pltpu
from jax.sharding import PartitionSpec as P

R = 8
STEPS = 4
HD = 128
GROUP = 7
ROWS = 32
BLOCK = 512
NBLK = 64
COUNT = 32
G = 8
NCHUNK = NBLK // G
FLOOR = -1e30
RATE = math.log2(math.e) / math.sqrt(HD)
MESH = pl.DeviceIdType.MESH


def kernel(
    q_hbm, k_hbm, v_hbm, nk_hbm, nv_hbm, len_hbm, req_hbm, idx_hbm, out_ref,
    kb, vb, sb, sm, sl, sa, top, qrow, qbuf, qs, nk, nv, msg, part,
    clen, req, idx, prev, ksem, vsem, small, q_send, q_recv, p_send, p_recv,
):
    me = lax.axis_index("seq")

    barrier = pltpu.get_barrier_semaphore()
    for k in range(1, COUNT):
        pl.semaphore_signal(barrier, inc=1, device_id={"seq": me ^ k}, device_id_type=MESH)

    small_copies = [
        pltpu.make_async_copy(src, dst, small.at[i])
        for i, (src, dst) in enumerate(
            ((q_hbm, qrow), (req_hbm, req), (idx_hbm, idx), (len_hbm, clen), (nk_hbm, nk), (nv_hbm, nv))
        )
    ]
    for copy in small_copies:
        copy.start()

    def k_copy(i):
        rows = pl.ds(i * G, G)
        return pltpu.make_async_copy(k_hbm.at[rows], kb.at[rows], ksem.at[i])

    def v_copy(i):
        rows = pl.ds(i * G, G)
        return pltpu.make_async_copy(v_hbm.at[rows], vb.at[rows], vsem.at[i])

    for i in range(NCHUNK):
        k_copy(i).start()
    for i in range(NCHUNK):
        v_copy(i).start()

    small_copies[0].wait()
    own = qrow[...].astype(jnp.float32)
    own = jnp.concatenate(
        [own[:, g * HD : (g + 1) * HD] for g in range(GROUP)] + [jnp.zeros((1, HD), jnp.float32)],
        axis=0,
    )
    qbuf[me] = own.astype(jnp.bfloat16)
    pl.semaphore_wait(barrier, COUNT - 1)
    for k in range(1, COUNT):
        pltpu.make_async_remote_copy(
            src_ref=qbuf.at[me],
            dst_ref=qbuf.at[me],
            send_sem=q_send,
            recv_sem=q_recv,
            device_id={"seq": me ^ k},
            device_id_type=MESH,
        ).start()

    for copy in small_copies[1:]:
        copy.wait()
    sm[0] = jnp.full((ROWS, HD), FLOOR, jnp.float32)
    sl[0] = jnp.zeros((ROWS, HD), jnp.float32)
    sa[0] = jnp.zeros((ROWS, HD), jnp.float32)

    def link(b, last):
        r = req[b]
        before = last[0]
        for j in range(1, R):
            before = jnp.where(r == j, last[j], before)
        prev[b] = before
        return tuple(jnp.where(r == j, b + 1, last[j]) for j in range(R))

    last = lax.fori_loop(0, NBLK, link, tuple(jnp.int32(0) for _ in range(R)))

    lane8 = lax.broadcasted_iota(jnp.int32, (8, HD), 1)
    row8 = lax.broadcasted_iota(jnp.int32, (8, HD), 0)

    own_request = me // STEPS
    own_step = me % STEPS
    fresh_k = nk[own_request].astype(jnp.float32)
    fresh_v = nv[own_request].astype(jnp.float32)
    fresh_s = []
    for u in range(STEPS):
        s = jnp.sum(own * fresh_k[u : u + 1, :], axis=1, keepdims=True)
        fresh_s.append(jnp.where(u <= own_step, jnp.broadcast_to(s, (8, HD)), FLOOR))
    fresh_m = fresh_s[0]
    for u in range(1, STEPS):
        fresh_m = jnp.maximum(fresh_m, fresh_s[u])
    fresh_l = jnp.zeros((8, HD), jnp.float32)
    fresh_a = jnp.zeros((8, HD), jnp.float32)
    for u in range(STEPS):
        w = jnp.exp2((fresh_s[u] - fresh_m) * RATE).astype(jnp.bfloat16).astype(jnp.float32)
        fresh_l = fresh_l + w
        fresh_a = fresh_a + w * fresh_v[u : u + 1, :]

    def stats(m, l):
        picked = jnp.where(lane8 == row8, m, jnp.where(lane8 == row8 + 8, l, 0.0))
        return jnp.sum(picked, axis=0, keepdims=True)

    fresh_row = stats(fresh_m, fresh_l)

    others = qbuf.at[pl.ds(0, COUNT - 1)]
    pltpu.make_async_copy(others, others, q_recv).wait()
    for r in range(R):
        qs[r] = qbuf[r * STEPS : (r + 1) * STEPS].astype(jnp.float32).reshape(ROWS, HD).astype(jnp.bfloat16)

    lane = lax.broadcasted_iota(jnp.int32, (ROWS, HD), 1)
    zero = jnp.zeros((ROWS, HD), jnp.bfloat16)

    def score_pair(b):
        q0 = qs[req[b]]
        q1 = qs[req[b + 1]]
        lhs = jnp.concatenate(
            [jnp.concatenate([q0, zero], axis=1), jnp.concatenate([zero, q1], axis=1)], axis=0
        )
        keys = jnp.concatenate([kb[b], kb[b + 1]], axis=1)
        s = lax.dot_general(lhs, keys, (((1,), (1,)), ((), ())), preferred_element_type=jnp.float32)
        for j in range(2):
            limit = clen[req[b + j]] - idx[b + j] * BLOCK
            most = None
            for t in range(0, BLOCK, HD):
                x = jnp.where(lane < limit - t, s[ROWS * j : ROWS * (j + 1), t : t + HD], FLOOR)
                sb[b + j, :, t : t + HD] = x
                most = x if most is None else jnp.maximum(most, x)
            sm[b + j + 1] = jnp.maximum(sm[prev[b + j]], most)

    def value_pair(b):
        weights = []
        for j in range(2):
            best = top[req[b + j]]
            total = None
            parts = []
            for t in range(0, BLOCK, HD):
                w = jnp.exp2((sb[b + j, :, t : t + HD] - best) * RATE)
                total = w if total is None else total + w
                parts.append(w.astype(jnp.bfloat16))
            sl[b + j + 1] = sl[prev[b + j]] + total
            weights.append(jnp.concatenate(parts, axis=1))
        lhs = jnp.concatenate(weights, axis=0)
        vals = jnp.concatenate([vb[b], vb[b + 1]], axis=1)
        o = lax.dot_general(lhs, vals, (((1,), (0,)), ((), ())), preferred_element_type=jnp.float32)
        sa[b + 1] = sa[prev[b]] + o[:ROWS, :HD]
        sa[b + 2] = sa[prev[b + 1]] + o[ROWS:, HD:]

    def score_chunk(i, _):
        k_copy(i).wait()
        for u in range(0, G, 2):
            score_pair(i * G + u)
        return 0

    lax.fori_loop(0, NCHUNK, score_chunk, 0)

    for r in range(R):
        top[r] = jnp.broadcast_to(jnp.max(sm[last[r]], axis=1, keepdims=True), (ROWS, HD))

    def value_chunk(i, _):
        v_copy(i).wait()
        for u in range(0, G, 2):
            value_pair(i * G + u)
        return 0

    lax.fori_loop(0, NCHUNK, value_chunk, 0)

    for r in range(R):
        m = top[r]
        l = jnp.broadcast_to(jnp.sum(sl[last[r]], axis=1, keepdims=True), (ROWS, HD))
        a = sa[last[r]]
        for s in range(STEPS):
            rows = slice(s * 8, s * 8 + 8)
            msg[r * STEPS + s] = jnp.where(row8 == 7, stats(m[rows], l[rows]), a[rows])
    for k in range(1, COUNT):
        pltpu.make_async_remote_copy(
            src_ref=msg.at[me ^ k],
            dst_ref=part.at[me],
            send_sem=p_send,
            recv_sem=p_recv,
            device_id={"seq": me ^ k},
            device_id_type=MESH,
        ).start()
    part[me] = msg[me]
    others = part.at[pl.ds(0, COUNT - 1)]
    pltpu.make_async_copy(others, others, p_recv).wait()

    rows = part[:, 7, :]
    best = jnp.maximum(jnp.max(rows, axis=0, keepdims=True), fresh_row)
    w = jnp.exp2((rows - best) * RATE)
    fresh_w = jnp.exp2((fresh_row - best) * RATE)
    total = jnp.sum(w * pltpu.roll(rows, HD - 8, 1), axis=0, keepdims=True)
    total = total + fresh_w * pltpu.roll(fresh_row, HD - 8, 1)
    w = w / total
    fresh_w = fresh_w / total

    def spread(row):
        picked = jnp.where(lane8 == row8, jnp.broadcast_to(row, (8, HD)), 0.0)
        return jnp.sum(picked, axis=1, keepdims=True)

    out = spread(fresh_w) * fresh_a
    for i in range(COUNT):
        out = out + spread(w[i : i + 1, :]) * part[i]
    out_ref[...] = jnp.concatenate([out[g : g + 1, :] for g in range(GROUP)], axis=1).astype(jnp.bfloat16)

    sent = qbuf.at[pl.ds(0, COUNT - 1)]
    pltpu.make_async_copy(sent, sent, q_send).wait()
    sent = msg.at[pl.ds(0, COUNT - 1)]
    pltpu.make_async_copy(sent, sent, p_send).wait()


def shards(queries, keys, values, new_keys, new_values, cache_len, block_request, block_index):
    f32, bf16, i32 = jnp.float32, jnp.bfloat16, jnp.int32
    dma = pltpu.SemaphoreType.DMA
    return pl.pallas_call(
        kernel,
        out_shape=jax.ShapeDtypeStruct((1, GROUP * HD), bf16),
        in_specs=[pl.BlockSpec(memory_space=pltpu.HBM)] * 8,
        out_specs=pl.BlockSpec(memory_space=pltpu.VMEM),
        scratch_shapes=[
            pltpu.VMEM((NBLK, BLOCK, HD), bf16),
            pltpu.VMEM((NBLK, BLOCK, HD), bf16),
            pltpu.VMEM((NBLK, ROWS, BLOCK), f32),
            pltpu.VMEM((NBLK + 1, ROWS, HD), f32),
            pltpu.VMEM((NBLK + 1, ROWS, HD), f32),
            pltpu.VMEM((NBLK + 1, ROWS, HD), f32),
            pltpu.VMEM((R, ROWS, HD), f32),
            pltpu.VMEM((1, GROUP * HD), bf16),
            pltpu.VMEM((COUNT, 8, HD), bf16),
            pltpu.VMEM((R, ROWS, HD), bf16),
            pltpu.VMEM((R, STEPS, HD), bf16),
            pltpu.VMEM((R, STEPS, HD), bf16),
            pltpu.VMEM((COUNT, 8, HD), f32),
            pltpu.VMEM((COUNT, 8, HD), f32),
            pltpu.SMEM((R,), i32),
            pltpu.SMEM((NBLK,), i32),
            pltpu.SMEM((NBLK,), i32),
            pltpu.SMEM((NBLK,), i32),
            dma((NCHUNK,)),
            dma((NCHUNK,)),
            dma((6,)),
            dma,
            dma,
            dma,
            dma,
        ],
        compiler_params=pltpu.CompilerParams(
            collective_id=0, has_side_effects=True, vmem_limit_bytes=63 * 2**20
        ),
        name="attend",
    )(queries, keys, values, new_keys, new_values, cache_len, block_request, block_index)


def solution(mesh):
    return jax.shard_map(
        shards,
        mesh=mesh,
        in_specs=(
            P("seq", "kvh"),
            P("seq", None, "kvh"),
            P("seq", None, "kvh"),
            P(None, None, "kvh"),
            P(None, None, "kvh"),
            P(),
            P("seq"),
            P("seq"),
        ),
        out_specs=P("seq", "kvh"),
        check_vma=False,
    )
```

```python
import math

import jax
import jax.numpy as jnp
from jax import lax
from jax.experimental import pallas as pl
from jax.experimental.pallas import tpu as pltpu
from jax.sharding import PartitionSpec as P

R = 8
STEPS = 4
HD = 128
GROUP = 7
ROWS = 32
BLOCK = 512
NBLK = 64
COUNT = 32
G = 32
NCHUNK = NBLK // G
FLOOR = -1e30
RATE = math.log2(math.e) / math.sqrt(HD)
MESH = pl.DeviceIdType.MESH


def hops(k):
    ring = (0, 1, 2, 1)
    return k // 16 + ring[k // 4 % 4] + ring[k % 4]


PEERS = sorted(range(1, COUNT), key=hops, reverse=True)


def kernel(
    q_hbm, k_hbm, v_hbm, nk_hbm, nv_hbm, len_hbm, req_hbm, idx_hbm, out_ref,
    kb, vb, sb, sm, sl, sa, top, qrow, qbuf, qs, nk, nv, msg, part,
    clen, req, idx, prev, ksem, vsem, small, q_send, q_recv, p_send, p_recv,
):
    me = lax.axis_index("seq")

    barrier = pltpu.get_barrier_semaphore()
    for k in PEERS:
        pl.semaphore_signal(barrier, inc=1, device_id={"seq": me ^ k}, device_id_type=MESH)

    small_copies = [
        pltpu.make_async_copy(src, dst, small.at[i])
        for i, (src, dst) in enumerate(
            ((q_hbm, qrow), (req_hbm, req), (idx_hbm, idx), (len_hbm, clen), (nk_hbm, nk), (nv_hbm, nv))
        )
    ]
    for copy in small_copies:
        copy.start()

    def k_copy(i):
        rows = pl.ds(i * G, G)
        return pltpu.make_async_copy(k_hbm.at[rows], kb.at[rows], ksem.at[i])

    def v_copy(i):
        rows = pl.ds(i * G, G)
        return pltpu.make_async_copy(v_hbm.at[rows], vb.at[rows], vsem.at[i])

    for i in range(NCHUNK):
        k_copy(i).start()
    for i in range(NCHUNK):
        v_copy(i).start()

    small_copies[0].wait()
    own = qrow[...].astype(jnp.float32)
    own = jnp.concatenate(
        [own[:, g * HD : (g + 1) * HD] for g in range(GROUP)] + [jnp.zeros((1, HD), jnp.float32)],
        axis=0,
    )
    qbuf[me] = own.astype(jnp.bfloat16)
    pl.semaphore_wait(barrier, COUNT - 1)
    for k in PEERS:
        pltpu.make_async_remote_copy(
            src_ref=qbuf.at[me],
            dst_ref=qbuf.at[me],
            send_sem=q_send,
            recv_sem=q_recv,
            device_id={"seq": me ^ k},
            device_id_type=MESH,
        ).start()

    for copy in small_copies[1:]:
        copy.wait()
    sm[0] = jnp.full((ROWS, HD), FLOOR, jnp.float32)
    sl[0] = jnp.zeros((ROWS, HD), jnp.float32)
    sa[0] = jnp.zeros((ROWS, HD), jnp.float32)

    def link(b, last):
        r = req[b]
        before = last[0]
        for j in range(1, R):
            before = jnp.where(r == j, last[j], before)
        prev[b] = before
        return tuple(jnp.where(r == j, b + 1, last[j]) for j in range(R))

    last = lax.fori_loop(0, NBLK, link, tuple(jnp.int32(0) for _ in range(R)))

    lane8 = lax.broadcasted_iota(jnp.int32, (8, HD), 1)
    row8 = lax.broadcasted_iota(jnp.int32, (8, HD), 0)

    own_request = me // STEPS
    own_step = me % STEPS
    fresh_k = nk[own_request].astype(jnp.float32)
    fresh_v = nv[own_request].astype(jnp.float32)
    fresh_s = []
    for u in range(STEPS):
        s = jnp.sum(own * fresh_k[u : u + 1, :], axis=1, keepdims=True)
        fresh_s.append(jnp.where(u <= own_step, jnp.broadcast_to(s, (8, HD)), FLOOR))
    fresh_m = fresh_s[0]
    for u in range(1, STEPS):
        fresh_m = jnp.maximum(fresh_m, fresh_s[u])
    fresh_l = jnp.zeros((8, HD), jnp.float32)
    fresh_a = jnp.zeros((8, HD), jnp.float32)
    for u in range(STEPS):
        w = jnp.exp2((fresh_s[u] - fresh_m) * RATE).astype(jnp.bfloat16).astype(jnp.float32)
        fresh_l = fresh_l + w
        fresh_a = fresh_a + w * fresh_v[u : u + 1, :]

    def stats(m, l):
        picked = jnp.where(lane8 == row8, m, jnp.where(lane8 == row8 + 8, l, 0.0))
        return jnp.sum(picked, axis=0, keepdims=True)

    fresh_row = stats(fresh_m, fresh_l)

    others = qbuf.at[pl.ds(0, COUNT - 1)]
    pltpu.make_async_copy(others, others, q_recv).wait()
    for r in range(R):
        qs[r] = qbuf[r * STEPS : (r + 1) * STEPS].astype(jnp.float32).reshape(ROWS, HD).astype(jnp.bfloat16)

    lane = lax.broadcasted_iota(jnp.int32, (ROWS, HD), 1)
    zero = jnp.zeros((ROWS, HD), jnp.bfloat16)

    def score_pair(b):
        q0 = qs[req[b]]
        q1 = qs[req[b + 1]]
        lhs = jnp.concatenate(
            [jnp.concatenate([q0, zero], axis=1), jnp.concatenate([zero, q1], axis=1)], axis=0
        )
        keys = jnp.concatenate([kb[b], kb[b + 1]], axis=1)
        s = lax.dot_general(lhs, keys, (((1,), (1,)), ((), ())), preferred_element_type=jnp.float32)
        for j in range(2):
            limit = clen[req[b + j]] - idx[b + j] * BLOCK
            most = None
            for t in range(0, BLOCK, HD):
                x = jnp.where(lane < limit - t, s[ROWS * j : ROWS * (j + 1), t : t + HD], FLOOR)
                sb[b + j, :, t : t + HD] = x
                most = x if most is None else jnp.maximum(most, x)
            sm[b + j + 1] = jnp.maximum(sm[prev[b + j]], most)

    def value_pair(b):
        weights = []
        for j in range(2):
            best = top[req[b + j]]
            total = None
            parts = []
            for t in range(0, BLOCK, HD):
                w = jnp.exp2((sb[b + j, :, t : t + HD] - best) * RATE)
                total = w if total is None else total + w
                parts.append(w.astype(jnp.bfloat16))
            sl[b + j + 1] = sl[prev[b + j]] + total
            weights.append(jnp.concatenate(parts, axis=1))
        lhs = jnp.concatenate(weights, axis=0)
        vals = jnp.concatenate([vb[b], vb[b + 1]], axis=1)
        o = lax.dot_general(lhs, vals, (((1,), (0,)), ((), ())), preferred_element_type=jnp.float32)
        sa[b + 1] = sa[prev[b]] + o[:ROWS, :HD]
        sa[b + 2] = sa[prev[b + 1]] + o[ROWS:, HD:]

    def score_chunk(i, _):
        k_copy(i).wait()
        for u in range(0, G, 2):
            score_pair(i * G + u)
        return 0

    lax.fori_loop(0, NCHUNK, score_chunk, 0)

    for r in range(R):
        top[r] = jnp.broadcast_to(jnp.max(sm[last[r]], axis=1, keepdims=True), (ROWS, HD))

    def value_chunk(i, _):
        v_copy(i).wait()
        for u in range(0, G, 2):
            value_pair(i * G + u)
        return 0

    lax.fori_loop(0, NCHUNK, value_chunk, 0)

    for r in range(R):
        m = top[r]
        l = jnp.broadcast_to(jnp.sum(sl[last[r]], axis=1, keepdims=True), (ROWS, HD))
        a = sa[last[r]]
        for s in range(STEPS):
            rows = slice(s * 8, s * 8 + 8)
            msg[r * STEPS + s] = jnp.where(row8 == 7, stats(m[rows], l[rows]), a[rows])
    for k in PEERS:
        pltpu.make_async_remote_copy(
            src_ref=msg.at[me ^ k],
            dst_ref=part.at[me],
            send_sem=p_send,
            recv_sem=p_recv,
            device_id={"seq": me ^ k},
            device_id_type=MESH,
        ).start()
    part[me] = msg[me]
    others = part.at[pl.ds(0, COUNT - 1)]
    pltpu.make_async_copy(others, others, p_recv).wait()

    rows = part[:, 7, :]
    best = jnp.maximum(jnp.max(rows, axis=0, keepdims=True), fresh_row)
    w = jnp.exp2((rows - best) * RATE)
    fresh_w = jnp.exp2((fresh_row - best) * RATE)
    total = jnp.sum(w * pltpu.roll(rows, HD - 8, 1), axis=0, keepdims=True)
    total = total + fresh_w * pltpu.roll(fresh_row, HD - 8, 1)
    w = w / total
    fresh_w = fresh_w / total

    def spread(row):
        picked = jnp.where(lane8 == row8, jnp.broadcast_to(row, (8, HD)), 0.0)
        return jnp.sum(picked, axis=1, keepdims=True)

    out = spread(fresh_w) * fresh_a
    for i in range(COUNT):
        out = out + spread(w[i : i + 1, :]) * part[i]
    out_ref[...] = jnp.concatenate([out[g : g + 1, :] for g in range(GROUP)], axis=1).astype(jnp.bfloat16)

    sent = qbuf.at[pl.ds(0, COUNT - 1)]
    pltpu.make_async_copy(sent, sent, q_send).wait()
    sent = msg.at[pl.ds(0, COUNT - 1)]
    pltpu.make_async_copy(sent, sent, p_send).wait()


def shards(queries, keys, values, new_keys, new_values, cache_len, block_request, block_index):
    f32, bf16, i32 = jnp.float32, jnp.bfloat16, jnp.int32
    dma = pltpu.SemaphoreType.DMA
    return pl.pallas_call(
        kernel,
        out_shape=pltpu.VMEM((1, GROUP * HD), bf16),
        in_specs=[pl.BlockSpec(memory_space=pltpu.HBM)] * 8,
        out_specs=pl.BlockSpec(memory_space=pltpu.VMEM),
        scratch_shapes=[
            pltpu.VMEM((NBLK, BLOCK, HD), bf16),
            pltpu.VMEM((NBLK, BLOCK, HD), bf16),
            pltpu.VMEM((NBLK, ROWS, BLOCK), f32),
            pltpu.VMEM((NBLK + 1, ROWS, HD), f32),
            pltpu.VMEM((NBLK + 1, ROWS, HD), f32),
            pltpu.VMEM((NBLK + 1, ROWS, HD), f32),
            pltpu.VMEM((R, ROWS, HD), f32),
            pltpu.VMEM((1, GROUP * HD), bf16),
            pltpu.VMEM((COUNT, 8, HD), bf16),
            pltpu.VMEM((R, ROWS, HD), bf16),
            pltpu.VMEM((R, STEPS, HD), bf16),
            pltpu.VMEM((R, STEPS, HD), bf16),
            pltpu.VMEM((COUNT, 8, HD), f32),
            pltpu.VMEM((COUNT, 8, HD), f32),
            pltpu.SMEM((R,), i32),
            pltpu.SMEM((NBLK,), i32),
            pltpu.SMEM((NBLK,), i32),
            pltpu.SMEM((NBLK,), i32),
            dma((NCHUNK,)),
            dma((NCHUNK,)),
            dma((6,)),
            dma,
            dma,
            dma,
            dma,
        ],
        compiler_params=pltpu.CompilerParams(
            collective_id=0, has_side_effects=True, vmem_limit_bytes=63 * 2**20
        ),
        name="attend",
    )(queries, keys, values, new_keys, new_values, cache_len, block_request, block_index)


def solution(mesh):
    return jax.shard_map(
        shards,
        mesh=mesh,
        in_specs=(
            P("seq", "kvh"),
            P("seq", None, "kvh"),
            P("seq", None, "kvh"),
            P(None, None, "kvh"),
            P(None, None, "kvh"),
            P(),
            P("seq"),
            P("seq"),
        ),
        out_specs=P("seq", "kvh"),
        check_vma=False,
    )
```

```python
import math

import jax
import jax.numpy as jnp
from jax import lax
from jax.experimental import pallas as pl
from jax.experimental.pallas import tpu as pltpu
from jax.sharding import PartitionSpec as P

R = 8
STEPS = 4
HD = 128
GROUP = 7
ROWS = 32
BLOCK = 512
NBLK = 64
COUNT = 32
G = 32
TURNS = NBLK // G
CHUNK = 16
NCHUNK = NBLK // CHUNK
FLOOR = -1e30
RATE = math.log2(math.e) / math.sqrt(HD)
MESH = pl.DeviceIdType.MESH


def hops(k):
    ring = (0, 1, 2, 1)
    return k // 16 + ring[k // 4 % 4] + ring[k % 4]


PEERS = sorted(range(1, COUNT), key=hops, reverse=True)


def kernel(
    q_hbm, k_hbm, v_hbm, nk_hbm, nv_hbm, len_hbm, req_hbm, idx_hbm, out_ref,
    kb, vb, kt, sb, sm, sl, sa, top, qrow, qbuf, qs, nk, nv, msg, part,
    clen, req, idx, prev, ksem, vsem, small, q_send, q_recv, p_send, p_recv,
):
    me = lax.axis_index("seq")

    barrier = pltpu.get_barrier_semaphore()
    for k in PEERS:
        pl.semaphore_signal(barrier, inc=1, device_id={"seq": me ^ k}, device_id_type=MESH)

    small_copies = [
        pltpu.make_async_copy(src, dst, small.at[i])
        for i, (src, dst) in enumerate(
            ((q_hbm, qrow), (req_hbm, req), (idx_hbm, idx), (len_hbm, clen), (nk_hbm, nk), (nv_hbm, nv))
        )
    ]
    for copy in small_copies:
        copy.start()

    def k_copy(i):
        rows = pl.ds(i * CHUNK, CHUNK)
        return pltpu.make_async_copy(k_hbm.at[rows], kb.at[rows], ksem.at[i])

    def v_copy(i):
        rows = pl.ds(i * CHUNK, CHUNK)
        return pltpu.make_async_copy(v_hbm.at[rows], vb.at[rows], vsem.at[i])

    for i in range(NCHUNK):
        k_copy(i).start()
    for i in range(NCHUNK):
        v_copy(i).start()

    small_copies[0].wait()
    own = qrow[...].astype(jnp.float32)
    own = jnp.concatenate(
        [own[:, g * HD : (g + 1) * HD] for g in range(GROUP)] + [jnp.zeros((1, HD), jnp.float32)],
        axis=0,
    )
    qbuf[me] = own.astype(jnp.bfloat16)
    pl.semaphore_wait(barrier, COUNT - 1)
    for k in PEERS:
        pltpu.make_async_remote_copy(
            src_ref=qbuf.at[me],
            dst_ref=qbuf.at[me],
            send_sem=q_send,
            recv_sem=q_recv,
            device_id={"seq": me ^ k},
            device_id_type=MESH,
        ).start()

    for copy in small_copies[1:]:
        copy.wait()
    sm[0] = jnp.full((ROWS, HD), FLOOR, jnp.float32)
    sl[0] = jnp.zeros((ROWS, HD), jnp.float32)
    sa[0] = jnp.zeros((ROWS, HD), jnp.float32)

    def link(b, last):
        r = req[b]
        before = last[0]
        for j in range(1, R):
            before = jnp.where(r == j, last[j], before)
        prev[b] = before
        return tuple(jnp.where(r == j, b + 1, last[j]) for j in range(R))

    last = lax.fori_loop(0, NBLK, link, tuple(jnp.int32(0) for _ in range(R)))

    lane8 = lax.broadcasted_iota(jnp.int32, (8, HD), 1)
    row8 = lax.broadcasted_iota(jnp.int32, (8, HD), 0)

    own_request = me // STEPS
    own_step = me % STEPS
    fresh_k = nk[own_request].astype(jnp.float32)
    fresh_v = nv[own_request].astype(jnp.float32)
    fresh_s = []
    for u in range(STEPS):
        s = jnp.sum(own * fresh_k[u : u + 1, :], axis=1, keepdims=True)
        fresh_s.append(jnp.where(u <= own_step, jnp.broadcast_to(s, (8, HD)), FLOOR))
    fresh_m = fresh_s[0]
    for u in range(1, STEPS):
        fresh_m = jnp.maximum(fresh_m, fresh_s[u])
    fresh_l = jnp.zeros((8, HD), jnp.float32)
    fresh_a = jnp.zeros((8, HD), jnp.float32)
    for u in range(STEPS):
        w = jnp.exp2((fresh_s[u] - fresh_m) * RATE).astype(jnp.bfloat16).astype(jnp.float32)
        fresh_l = fresh_l + w
        fresh_a = fresh_a + w * fresh_v[u : u + 1, :]

    def turn(*columns):
        picked = 0.0
        for i, column in enumerate(columns):
            picked = jnp.where(lane8 == row8 + 8 * i, column, picked)
        return jnp.sum(picked, axis=0, keepdims=True)

    fresh_m_row = turn(fresh_m)
    fresh_l_row = turn(fresh_l)

    def turn_keys(i, _):
        for u in range(4):
            kt[i * 4 + u] = kb[i * 4 + u].T
        return 0

    for i in range(NCHUNK):
        k_copy(i).wait()
        lax.fori_loop(i * CHUNK // 4, (i + 1) * CHUNK // 4, turn_keys, 0)

    others = qbuf.at[pl.ds(0, COUNT - 1)]
    pltpu.make_async_copy(others, others, q_recv).wait()
    for r in range(R):
        qs[r] = qbuf[r * STEPS : (r + 1) * STEPS].astype(jnp.float32).reshape(ROWS, HD).astype(jnp.bfloat16)

    lane = lax.broadcasted_iota(jnp.int32, (ROWS, HD), 1)
    zero = jnp.zeros((ROWS, HD), jnp.bfloat16)

    def score_pair(b):
        q0 = qs[req[b]]
        q1 = qs[req[b + 1]]
        lhs = jnp.concatenate(
            [jnp.concatenate([q0, zero], axis=1), jnp.concatenate([zero, q1], axis=1)], axis=0
        )
        keys = jnp.concatenate([kt[b], kt[b + 1]], axis=0)
        s = lax.dot_general(lhs, keys, (((1,), (0,)), ((), ())), preferred_element_type=jnp.float32)
        for j in range(2):
            limit = clen[req[b + j]] - idx[b + j] * BLOCK
            most = None
            for t in range(0, BLOCK, HD):
                x = jnp.where(lane < limit - t, s[ROWS * j : ROWS * (j + 1), t : t + HD], FLOOR)
                sb[b + j, :, t : t + HD] = x
                most = x if most is None else jnp.maximum(most, x)
            sm[b + j + 1] = jnp.maximum(sm[prev[b + j]], most)

    def value_pair(b):
        weights = []
        for j in range(2):
            best = top[req[b + j]]
            total = None
            parts = []
            for t in range(0, BLOCK, HD):
                w = jnp.exp2((sb[b + j, :, t : t + HD] - best) * RATE)
                total = w if total is None else total + w
                parts.append(w.astype(jnp.bfloat16))
            sl[b + j + 1] = sl[prev[b + j]] + total
            weights.append(jnp.concatenate(parts, axis=1))
        lhs = jnp.concatenate(weights, axis=0)
        vals = jnp.concatenate([vb[b], vb[b + 1]], axis=1)
        o = lax.dot_general(lhs, vals, (((1,), (0,)), ((), ())), preferred_element_type=jnp.float32)
        sa[b + 1] = sa[prev[b]] + o[:ROWS, :HD]
        sa[b + 2] = sa[prev[b + 1]] + o[ROWS:, HD:]

    def score_turn(i, _):
        for u in range(0, G, 2):
            score_pair(i * G + u)
        return 0

    lax.fori_loop(0, TURNS, score_turn, 0)

    for r in range(R):
        top[r] = jnp.broadcast_to(jnp.max(sm[last[r]], axis=1, keepdims=True), (ROWS, HD))
    for i in range(NCHUNK):
        v_copy(i).wait()

    def value_turn(i, _):
        for u in range(0, G, 2):
            value_pair(i * G + u)
        return 0

    lax.fori_loop(0, TURNS, value_turn, 0)

    for r in range(R):
        m = top[r]
        l = jnp.broadcast_to(jnp.sum(sl[last[r]], axis=1, keepdims=True), (ROWS, HD))
        a = sa[last[r]]
        for s in range(STEPS):
            rows = slice(s * 8, s * 8 + 8)
            msg[r * STEPS + s] = jnp.where(row8 == 7, turn(m[rows], l[rows]), a[rows])
    for k in PEERS:
        pltpu.make_async_remote_copy(
            src_ref=msg.at[me ^ k],
            dst_ref=part.at[me],
            send_sem=p_send,
            recv_sem=p_recv,
            device_id={"seq": me ^ k},
            device_id_type=MESH,
        ).start()
    part[me] = msg[me]
    others = part.at[pl.ds(0, COUNT - 1)]
    pltpu.make_async_copy(others, others, p_recv).wait()

    m = part[:, 7, :]
    l = pltpu.roll(m, HD - 8, 1)
    best = jnp.maximum(jnp.max(m, axis=0, keepdims=True), fresh_m_row)
    w = jnp.exp2((m - best) * RATE)
    fresh_w = jnp.exp2((fresh_m_row - best) * RATE)
    total = jnp.sum(w * l, axis=0, keepdims=True) + fresh_w * fresh_l_row
    w = w / total
    fresh_w = fresh_w / total

    def spread(row):
        picked = jnp.where(lane8 == row8, jnp.broadcast_to(row, (8, HD)), 0.0)
        return jnp.sum(picked, axis=1, keepdims=True)

    out = spread(fresh_w) * fresh_a
    for i in range(COUNT):
        out = out + spread(w[i : i + 1, :]) * part[i]
    out_ref[...] = jnp.concatenate([out[g : g + 1, :] for g in range(GROUP)], axis=1).astype(jnp.bfloat16)

    sent = qbuf.at[pl.ds(0, COUNT - 1)]
    pltpu.make_async_copy(sent, sent, q_send).wait()
    sent = msg.at[pl.ds(0, COUNT - 1)]
    pltpu.make_async_copy(sent, sent, p_send).wait()


def shards(queries, keys, values, new_keys, new_values, cache_len, block_request, block_index):
    f32, bf16, i32 = jnp.float32, jnp.bfloat16, jnp.int32
    dma = pltpu.SemaphoreType.DMA
    return pl.pallas_call(
        kernel,
        out_shape=pltpu.VMEM((1, GROUP * HD), bf16),
        in_specs=[pl.BlockSpec(memory_space=pltpu.HBM)] * 8,
        out_specs=pl.BlockSpec(memory_space=pltpu.VMEM),
        scratch_shapes=[
            pltpu.VMEM((NBLK, BLOCK, HD), bf16),
            pltpu.VMEM((NBLK, BLOCK, HD), bf16),
            pltpu.VMEM((NBLK, HD, BLOCK), bf16),
            pltpu.VMEM((NBLK, ROWS, BLOCK), f32),
            pltpu.VMEM((NBLK + 1, ROWS, HD), f32),
            pltpu.VMEM((NBLK + 1, ROWS, HD), f32),
            pltpu.VMEM((NBLK + 1, ROWS, HD), f32),
            pltpu.VMEM((R, ROWS, HD), f32),
            pltpu.VMEM((1, GROUP * HD), bf16),
            pltpu.VMEM((COUNT, 8, HD), bf16),
            pltpu.VMEM((R, ROWS, HD), bf16),
            pltpu.VMEM((R, STEPS, HD), bf16),
            pltpu.VMEM((R, STEPS, HD), bf16),
            pltpu.VMEM((COUNT, 8, HD), f32),
            pltpu.VMEM((COUNT, 8, HD), f32),
            pltpu.SMEM((R,), i32),
            pltpu.SMEM((NBLK,), i32),
            pltpu.SMEM((NBLK,), i32),
            pltpu.SMEM((NBLK,), i32),
            dma((NCHUNK,)),
            dma((NCHUNK,)),
            dma((6,)),
            dma,
            dma,
            dma,
            dma,
        ],
        compiler_params=pltpu.CompilerParams(
            collective_id=0, has_side_effects=True, vmem_limit_bytes=63 * 2**20
        ),
        name="attend",
    )(queries, keys, values, new_keys, new_values, cache_len, block_request, block_index)


def solution(mesh):
    return jax.shard_map(
        shards,
        mesh=mesh,
        in_specs=(
            P("seq", "kvh"),
            P("seq", None, "kvh"),
            P("seq", None, "kvh"),
            P(None, None, "kvh"),
            P(None, None, "kvh"),
            P(),
            P("seq"),
            P("seq"),
        ),
        out_specs=P("seq", "kvh"),
        check_vma=False,
    )
```

```python
import math

import jax
import jax.numpy as jnp
from jax import lax
from jax.experimental import pallas as pl
from jax.experimental.pallas import tpu as pltpu
from jax.sharding import PartitionSpec as P

R = 8
STEPS = 4
HD = 128
GROUP = 7
ROWS = 32
BLOCK = 512
NBLK = 64
COUNT = 32
G = 64
TURNS = NBLK // G
CHUNK = 16
NCHUNK = NBLK // CHUNK
FLOOR = -1e30
RATE = math.log2(math.e) / math.sqrt(HD)
MESH = pl.DeviceIdType.MESH


def hops(k):
    ring = (0, 1, 2, 1)
    return k // 16 + ring[k // 4 % 4] + ring[k % 4]


PEERS = sorted(range(1, COUNT), key=hops, reverse=True)


def kernel(
    q_hbm, k_hbm, v_hbm, nk_hbm, nv_hbm, len_hbm, req_hbm, idx_hbm, out_ref,
    kb, vb, kt, sb, sm, sl, sa, top, qrow, qbuf, qs, nk, nv, msg, part,
    clen, req, idx, prev, ksem, vsem, small, q_send, q_recv, p_send, p_recv,
):
    me = lax.axis_index("seq")

    barrier = pltpu.get_barrier_semaphore()
    for k in PEERS:
        pl.semaphore_signal(barrier, inc=1, device_id={"seq": me ^ k}, device_id_type=MESH)

    small_copies = [
        pltpu.make_async_copy(src, dst, small.at[i])
        for i, (src, dst) in enumerate(
            ((q_hbm, qrow), (req_hbm, req), (idx_hbm, idx), (len_hbm, clen), (nk_hbm, nk), (nv_hbm, nv))
        )
    ]
    for copy in small_copies:
        copy.start()

    def k_copy(i):
        rows = pl.ds(i * CHUNK, CHUNK)
        return pltpu.make_async_copy(k_hbm.at[rows], kb.at[rows], ksem.at[i])

    def v_copy(i):
        rows = pl.ds(i * CHUNK, CHUNK)
        return pltpu.make_async_copy(v_hbm.at[rows], vb.at[rows], vsem.at[i])

    for i in range(NCHUNK):
        k_copy(i).start()
    for i in range(NCHUNK):
        v_copy(i).start()

    small_copies[0].wait()
    own = qrow[...].astype(jnp.float32)
    own = jnp.concatenate(
        [own[:, g * HD : (g + 1) * HD] for g in range(GROUP)] + [jnp.zeros((1, HD), jnp.float32)],
        axis=0,
    )
    qbuf[me] = own.astype(jnp.bfloat16)
    pl.semaphore_wait(barrier, COUNT - 1)
    for k in PEERS:
        pltpu.make_async_remote_copy(
            src_ref=qbuf.at[me],
            dst_ref=qbuf.at[me],
            send_sem=q_send,
            recv_sem=q_recv,
            device_id={"seq": me ^ k},
            device_id_type=MESH,
        ).start()

    for copy in small_copies[1:]:
        copy.wait()
    sm[0] = jnp.full((ROWS, HD), FLOOR, jnp.float32)
    sl[0] = jnp.zeros((ROWS, HD), jnp.float32)
    sa[0] = jnp.zeros((ROWS, HD), jnp.float32)

    def link(b, last):
        r = req[b]
        before = last[0]
        for j in range(1, R):
            before = jnp.where(r == j, last[j], before)
        prev[b] = before
        return tuple(jnp.where(r == j, b + 1, last[j]) for j in range(R))

    last = lax.fori_loop(0, NBLK, link, tuple(jnp.int32(0) for _ in range(R)))

    lane8 = lax.broadcasted_iota(jnp.int32, (8, HD), 1)
    row8 = lax.broadcasted_iota(jnp.int32, (8, HD), 0)

    own_request = me // STEPS
    own_step = me % STEPS
    fresh_k = nk[own_request].astype(jnp.float32)
    fresh_v = nv[own_request].astype(jnp.float32)
    fresh_s = []
    for u in range(STEPS):
        s = jnp.sum(own * fresh_k[u : u + 1, :], axis=1, keepdims=True)
        fresh_s.append(jnp.where(u <= own_step, jnp.broadcast_to(s, (8, HD)), FLOOR))
    fresh_m = fresh_s[0]
    for u in range(1, STEPS):
        fresh_m = jnp.maximum(fresh_m, fresh_s[u])
    fresh_l = jnp.zeros((8, HD), jnp.float32)
    fresh_a = jnp.zeros((8, HD), jnp.float32)
    for u in range(STEPS):
        w = jnp.exp2((fresh_s[u] - fresh_m) * RATE).astype(jnp.bfloat16).astype(jnp.float32)
        fresh_l = fresh_l + w
        fresh_a = fresh_a + w * fresh_v[u : u + 1, :]

    def turn(*columns):
        picked = 0.0
        for i, column in enumerate(columns):
            picked = jnp.where(lane8 == row8 + 8 * i, column, picked)
        return jnp.sum(picked, axis=0, keepdims=True)

    fresh_m_row = turn(fresh_m)
    fresh_l_row = turn(fresh_l)

    def turn_keys(i, _):
        for u in range(4):
            kt[i * 4 + u] = kb[i * 4 + u].T
        return 0

    for i in range(NCHUNK):
        k_copy(i).wait()
        lax.fori_loop(i * CHUNK // 4, (i + 1) * CHUNK // 4, turn_keys, 0)

    others = qbuf.at[pl.ds(0, COUNT - 1)]
    pltpu.make_async_copy(others, others, q_recv).wait()
    for r in range(R):
        qs[r] = qbuf[r * STEPS : (r + 1) * STEPS].astype(jnp.float32).reshape(ROWS, HD).astype(jnp.bfloat16)

    lane = lax.broadcasted_iota(jnp.int32, (ROWS, HD), 1)
    zero = jnp.zeros((ROWS, HD), jnp.bfloat16)

    def score_pair(b):
        q0 = qs[req[b]]
        q1 = qs[req[b + 1]]
        lhs = jnp.concatenate(
            [jnp.concatenate([q0, zero], axis=1), jnp.concatenate([zero, q1], axis=1)], axis=0
        )
        keys = jnp.concatenate([kt[b], kt[b + 1]], axis=0)
        s = lax.dot_general(lhs, keys, (((1,), (0,)), ((), ())), preferred_element_type=jnp.float32)
        for j in range(2):
            limit = clen[req[b + j]] - idx[b + j] * BLOCK
            most = None
            for t in range(0, BLOCK, HD):
                x = jnp.where(lane < limit - t, s[ROWS * j : ROWS * (j + 1), t : t + HD], FLOOR)
                sb[b + j, :, t : t + HD] = x
                most = x if most is None else jnp.maximum(most, x)
            sm[b + j + 1] = jnp.maximum(sm[prev[b + j]], most)

    def value_pair(b):
        weights = []
        for j in range(2):
            best = top[req[b + j]]
            total = None
            parts = []
            for t in range(0, BLOCK, HD):
                w = jnp.exp2((sb[b + j, :, t : t + HD] - best) * RATE)
                total = w if total is None else total + w
                parts.append(w.astype(jnp.bfloat16))
            sl[b + j + 1] = sl[prev[b + j]] + total
            weights.append(jnp.concatenate(parts, axis=1))
        lhs = jnp.concatenate(weights, axis=0)
        vals = jnp.concatenate([vb[b], vb[b + 1]], axis=1)
        o = lax.dot_general(lhs, vals, (((1,), (0,)), ((), ())), preferred_element_type=jnp.float32)
        sa[b + 1] = sa[prev[b]] + o[:ROWS, :HD]
        sa[b + 2] = sa[prev[b + 1]] + o[ROWS:, HD:]

    def score_turn(i, _):
        for u in range(0, G, 2):
            score_pair(i * G + u)
        return 0

    lax.fori_loop(0, TURNS, score_turn, 0)

    for r in range(R):
        top[r] = jnp.broadcast_to(jnp.max(sm[last[r]], axis=1, keepdims=True), (ROWS, HD))
    for i in range(NCHUNK):
        v_copy(i).wait()

    def value_turn(i, _):
        for u in range(0, G, 2):
            value_pair(i * G + u)
        return 0

    lax.fori_loop(0, TURNS, value_turn, 0)

    for r in range(R):
        m = top[r]
        l = jnp.broadcast_to(jnp.sum(sl[last[r]], axis=1, keepdims=True), (ROWS, HD))
        a = sa[last[r]]
        for s in range(STEPS):
            rows = slice(s * 8, s * 8 + 8)
            msg[r * STEPS + s] = jnp.where(row8 == 7, turn(m[rows], l[rows]), a[rows])
    for k in PEERS:
        pltpu.make_async_remote_copy(
            src_ref=msg.at[me ^ k],
            dst_ref=part.at[me],
            send_sem=p_send,
            recv_sem=p_recv,
            device_id={"seq": me ^ k},
            device_id_type=MESH,
        ).start()
    part[me] = msg[me]
    others = part.at[pl.ds(0, COUNT - 1)]
    pltpu.make_async_copy(others, others, p_recv).wait()

    m = part[:, 7, :]
    l = pltpu.roll(m, HD - 8, 1)
    best = jnp.maximum(jnp.max(m, axis=0, keepdims=True), fresh_m_row)
    w = jnp.exp2((m - best) * RATE)
    fresh_w = jnp.exp2((fresh_m_row - best) * RATE)
    total = jnp.sum(w * l, axis=0, keepdims=True) + fresh_w * fresh_l_row
    w = w / total
    fresh_w = fresh_w / total

    def spread(row):
        picked = jnp.where(lane8 == row8, jnp.broadcast_to(row, (8, HD)), 0.0)
        return jnp.sum(picked, axis=1, keepdims=True)

    out = spread(fresh_w) * fresh_a
    for i in range(COUNT):
        out = out + spread(w[i : i + 1, :]) * part[i]
    out_ref[...] = jnp.concatenate([out[g : g + 1, :] for g in range(GROUP)], axis=1).astype(jnp.bfloat16)

    sent = qbuf.at[pl.ds(0, COUNT - 1)]
    pltpu.make_async_copy(sent, sent, q_send).wait()
    sent = msg.at[pl.ds(0, COUNT - 1)]
    pltpu.make_async_copy(sent, sent, p_send).wait()


def shards(queries, keys, values, new_keys, new_values, cache_len, block_request, block_index):
    f32, bf16, i32 = jnp.float32, jnp.bfloat16, jnp.int32
    dma = pltpu.SemaphoreType.DMA
    return pl.pallas_call(
        kernel,
        out_shape=pltpu.VMEM((1, GROUP * HD), bf16),
        in_specs=[pl.BlockSpec(memory_space=pltpu.HBM)] * 8,
        out_specs=pl.BlockSpec(memory_space=pltpu.VMEM),
        scratch_shapes=[
            pltpu.VMEM((NBLK, BLOCK, HD), bf16),
            pltpu.VMEM((NBLK, BLOCK, HD), bf16),
            pltpu.VMEM((NBLK, HD, BLOCK), bf16),
            pltpu.VMEM((NBLK, ROWS, BLOCK), f32),
            pltpu.VMEM((NBLK + 1, ROWS, HD), f32),
            pltpu.VMEM((NBLK + 1, ROWS, HD), f32),
            pltpu.VMEM((NBLK + 1, ROWS, HD), f32),
            pltpu.VMEM((R, ROWS, HD), f32),
            pltpu.VMEM((1, GROUP * HD), bf16),
            pltpu.VMEM((COUNT, 8, HD), bf16),
            pltpu.VMEM((R, ROWS, HD), bf16),
            pltpu.VMEM((R, STEPS, HD), bf16),
            pltpu.VMEM((R, STEPS, HD), bf16),
            pltpu.VMEM((COUNT, 8, HD), f32),
            pltpu.VMEM((COUNT, 8, HD), f32),
            pltpu.SMEM((R,), i32),
            pltpu.SMEM((NBLK,), i32),
            pltpu.SMEM((NBLK,), i32),
            pltpu.SMEM((NBLK,), i32),
            dma((NCHUNK,)),
            dma((NCHUNK,)),
            dma((6,)),
            dma,
            dma,
            dma,
            dma,
        ],
        compiler_params=pltpu.CompilerParams(
            collective_id=0, has_side_effects=True, vmem_limit_bytes=63 * 2**20
        ),
        name="attend",
    )(queries, keys, values, new_keys, new_values, cache_len, block_request, block_index)


def solution(mesh):
    return jax.shard_map(
        shards,
        mesh=mesh,
        in_specs=(
            P("seq", "kvh"),
            P("seq", None, "kvh"),
            P("seq", None, "kvh"),
            P(None, None, "kvh"),
            P(None, None, "kvh"),
            P(),
            P("seq"),
            P("seq"),
        ),
        out_specs=P("seq", "kvh"),
        check_vma=False,
    )
```

```python
import math

import jax
import jax.numpy as jnp
from jax import lax
from jax.experimental import pallas as pl
from jax.experimental.pallas import tpu as pltpu
from jax.sharding import PartitionSpec as P

R = 8
STEPS = 4
HD = 128
GROUP = 7
ROWS = 32
BLOCK = 512
NBLK = 64
COUNT = 32
CHUNK = 16
NCHUNK = NBLK // CHUNK
FLOOR = -1e30
RATE = math.log2(math.e) / math.sqrt(HD)
MESH = pl.DeviceIdType.MESH


def hops(k):
    ring = (0, 1, 2, 1)
    return k // 16 + ring[k // 4 % 4] + ring[k % 4]


PEERS = sorted(range(1, COUNT), key=hops, reverse=True)


def kernel(
    q_hbm, k_hbm, v_hbm, nk_hbm, nv_hbm, len_hbm, req_hbm, idx_hbm, out_ref,
    kb, vb, kt, sb, sm, sl, sa, top, qrow, qbuf, qs, nk, nv, msg, part,
    clen, req, idx, prev, ksem, vsem, small, q_send, q_recv, p_send, p_recv,
):
    me = lax.axis_index("seq")

    barrier = pltpu.get_barrier_semaphore()
    for k in PEERS:
        pl.semaphore_signal(barrier, inc=1, device_id={"seq": me ^ k}, device_id_type=MESH)

    small_copies = [
        pltpu.make_async_copy(src, dst, small.at[i])
        for i, (src, dst) in enumerate(
            ((q_hbm, qrow), (req_hbm, req), (idx_hbm, idx), (len_hbm, clen), (nk_hbm, nk), (nv_hbm, nv))
        )
    ]
    for copy in small_copies:
        copy.start()

    def k_copy(i):
        rows = pl.ds(i * CHUNK, CHUNK)
        return pltpu.make_async_copy(k_hbm.at[rows], kb.at[rows], ksem.at[i])

    def v_copy(i):
        rows = pl.ds(i * CHUNK, CHUNK)
        return pltpu.make_async_copy(v_hbm.at[rows], vb.at[rows], vsem.at[i])

    for i in range(NCHUNK):
        k_copy(i).start()
    for i in range(NCHUNK):
        v_copy(i).start()

    small_copies[0].wait()
    own = qrow[...].astype(jnp.float32)
    own = jnp.concatenate(
        [own[:, g * HD : (g + 1) * HD] for g in range(GROUP)] + [jnp.zeros((1, HD), jnp.float32)],
        axis=0,
    )
    qbuf[me] = own.astype(jnp.bfloat16)
    pl.semaphore_wait(barrier, COUNT - 1)
    for k in PEERS:
        pltpu.make_async_remote_copy(
            src_ref=qbuf.at[me],
            dst_ref=qbuf.at[me],
            send_sem=q_send,
            recv_sem=q_recv,
            device_id={"seq": me ^ k},
            device_id_type=MESH,
        ).start()

    for copy in small_copies[1:]:
        copy.wait()
    sm[0] = jnp.full((ROWS, HD), FLOOR, jnp.float32)
    sl[0] = jnp.zeros((ROWS, HD), jnp.float32)
    sa[0] = jnp.zeros((ROWS, HD), jnp.float32)

    def link(b, last):
        r = req[b]
        before = last[0]
        for j in range(1, R):
            before = jnp.where(r == j, last[j], before)
        prev[b] = before
        return tuple(jnp.where(r == j, b + 1, last[j]) for j in range(R))

    last = lax.fori_loop(0, NBLK, link, tuple(jnp.int32(0) for _ in range(R)))

    lane8 = lax.broadcasted_iota(jnp.int32, (8, HD), 1)
    row8 = lax.broadcasted_iota(jnp.int32, (8, HD), 0)

    own_request = me // STEPS
    own_step = me % STEPS
    fresh_k = nk[own_request].astype(jnp.float32)
    fresh_v = nv[own_request].astype(jnp.float32)
    fresh_s = []
    for u in range(STEPS):
        s = jnp.sum(own * fresh_k[u : u + 1, :], axis=1, keepdims=True)
        fresh_s.append(jnp.where(u <= own_step, jnp.broadcast_to(s, (8, HD)), FLOOR))
    fresh_m = fresh_s[0]
    for u in range(1, STEPS):
        fresh_m = jnp.maximum(fresh_m, fresh_s[u])
    fresh_l = jnp.zeros((8, HD), jnp.float32)
    fresh_a = jnp.zeros((8, HD), jnp.float32)
    for u in range(STEPS):
        w = jnp.exp2((fresh_s[u] - fresh_m) * RATE).astype(jnp.bfloat16).astype(jnp.float32)
        fresh_l = fresh_l + w
        fresh_a = fresh_a + w * fresh_v[u : u + 1, :]

    def turn(*columns):
        picked = 0.0
        for i, column in enumerate(columns):
            picked = jnp.where(lane8 == row8 + 8 * i, column, picked)
        return jnp.sum(picked, axis=0, keepdims=True)

    fresh_m_row = turn(fresh_m)
    fresh_l_row = turn(fresh_l)

    def turn_keys(i, _):
        for u in range(4):
            kt[i * 4 + u] = kb[i * 4 + u].T
        return 0

    for i in range(NCHUNK):
        k_copy(i).wait()
        lax.fori_loop(i * CHUNK // 4, (i + 1) * CHUNK // 4, turn_keys, 0)

    others = qbuf.at[pl.ds(0, COUNT - 1)]
    pltpu.make_async_copy(others, others, q_recv).wait()
    for r in range(R):
        qs[r] = qbuf[r * STEPS : (r + 1) * STEPS].astype(jnp.float32).reshape(ROWS, HD).astype(jnp.bfloat16)

    lane = lax.broadcasted_iota(jnp.int32, (ROWS, HD), 1)

    for b in range(NBLK):
        s = jnp.dot(qs[req[b]], kt[b], preferred_element_type=jnp.float32)
        limit = clen[req[b]] - idx[b] * BLOCK
        most = None
        for t in range(0, BLOCK, HD):
            x = jnp.where(lane < limit - t, s[:, t : t + HD], FLOOR)
            sb[b, :, t : t + HD] = x
            most = x if most is None else jnp.maximum(most, x)
        sm[b + 1] = jnp.maximum(sm[prev[b]], most)

    for r in range(R):
        top[r] = jnp.broadcast_to(jnp.max(sm[last[r]], axis=1, keepdims=True), (ROWS, HD))
    for i in range(NCHUNK):
        v_copy(i).wait()

    for b in range(NBLK):
        best = top[req[b]]
        total = None
        parts = []
        for t in range(0, BLOCK, HD):
            w = jnp.exp2((sb[b, :, t : t + HD] - best) * RATE)
            total = w if total is None else total + w
            parts.append(w.astype(jnp.bfloat16))
        sl[b + 1] = sl[prev[b]] + total
        o = jnp.dot(jnp.concatenate(parts, axis=1), vb[b], preferred_element_type=jnp.float32)
        sa[b + 1] = sa[prev[b]] + o

    for r in range(R):
        m = top[r]
        l = jnp.broadcast_to(jnp.sum(sl[last[r]], axis=1, keepdims=True), (ROWS, HD))
        a = sa[last[r]]
        for s in range(STEPS):
            rows = slice(s * 8, s * 8 + 8)
            msg[r * STEPS + s] = jnp.where(row8 == 7, turn(m[rows], l[rows]), a[rows])
    for k in PEERS:
        pltpu.make_async_remote_copy(
            src_ref=msg.at[me ^ k],
            dst_ref=part.at[me],
            send_sem=p_send,
            recv_sem=p_recv,
            device_id={"seq": me ^ k},
            device_id_type=MESH,
        ).start()
    part[me] = msg[me]
    others = part.at[pl.ds(0, COUNT - 1)]
    pltpu.make_async_copy(others, others, p_recv).wait()

    m = part[:, 7, :]
    l = pltpu.roll(m, HD - 8, 1)
    best = jnp.maximum(jnp.max(m, axis=0, keepdims=True), fresh_m_row)
    w = jnp.exp2((m - best) * RATE)
    fresh_w = jnp.exp2((fresh_m_row - best) * RATE)
    total = jnp.sum(w * l, axis=0, keepdims=True) + fresh_w * fresh_l_row
    w = w / total
    fresh_w = fresh_w / total

    def spread(row):
        picked = jnp.where(lane8 == row8, jnp.broadcast_to(row, (8, HD)), 0.0)
        return jnp.sum(picked, axis=1, keepdims=True)

    out = spread(fresh_w) * fresh_a
    for i in range(COUNT):
        out = out + spread(w[i : i + 1, :]) * part[i]
    out_ref[...] = jnp.concatenate([out[g : g + 1, :] for g in range(GROUP)], axis=1).astype(jnp.bfloat16)

    sent = qbuf.at[pl.ds(0, COUNT - 1)]
    pltpu.make_async_copy(sent, sent, q_send).wait()
    sent = msg.at[pl.ds(0, COUNT - 1)]
    pltpu.make_async_copy(sent, sent, p_send).wait()


def shards(queries, keys, values, new_keys, new_values, cache_len, block_request, block_index):
    f32, bf16, i32 = jnp.float32, jnp.bfloat16, jnp.int32
    dma = pltpu.SemaphoreType.DMA
    return pl.pallas_call(
        kernel,
        out_shape=pltpu.VMEM((1, GROUP * HD), bf16),
        in_specs=[pl.BlockSpec(memory_space=pltpu.HBM)] * 8,
        out_specs=pl.BlockSpec(memory_space=pltpu.VMEM),
        scratch_shapes=[
            pltpu.VMEM((NBLK, BLOCK, HD), bf16),
            pltpu.VMEM((NBLK, BLOCK, HD), bf16),
            pltpu.VMEM((NBLK, HD, BLOCK), bf16),
            pltpu.VMEM((NBLK, ROWS, BLOCK), f32),
            pltpu.VMEM((NBLK + 1, ROWS, HD), f32),
            pltpu.VMEM((NBLK + 1, ROWS, HD), f32),
            pltpu.VMEM((NBLK + 1, ROWS, HD), f32),
            pltpu.VMEM((R, ROWS, HD), f32),
            pltpu.VMEM((1, GROUP * HD), bf16),
            pltpu.VMEM((COUNT, 8, HD), bf16),
            pltpu.VMEM((R, ROWS, HD), bf16),
            pltpu.VMEM((R, STEPS, HD), bf16),
            pltpu.VMEM((R, STEPS, HD), bf16),
            pltpu.VMEM((COUNT, 8, HD), f32),
            pltpu.VMEM((COUNT, 8, HD), f32),
            pltpu.SMEM((R,), i32),
            pltpu.SMEM((NBLK,), i32),
            pltpu.SMEM((NBLK,), i32),
            pltpu.SMEM((NBLK,), i32),
            dma((NCHUNK,)),
            dma((NCHUNK,)),
            dma((6,)),
            dma,
            dma,
            dma,
            dma,
        ],
        compiler_params=pltpu.CompilerParams(
            collective_id=0, has_side_effects=True, vmem_limit_bytes=63 * 2**20
        ),
        name="attend",
    )(queries, keys, values, new_keys, new_values, cache_len, block_request, block_index)


def solution(mesh):
    return jax.shard_map(
        shards,
        mesh=mesh,
        in_specs=(
            P("seq", "kvh"),
            P("seq", None, "kvh"),
            P("seq", None, "kvh"),
            P(None, None, "kvh"),
            P(None, None, "kvh"),
            P(),
            P("seq"),
            P("seq"),
        ),
        out_specs=P("seq", "kvh"),
        check_vma=False,
    )
```

```python
import math

import jax
import jax.numpy as jnp
from jax import lax
from jax.experimental import pallas as pl
from jax.experimental.pallas import tpu as pltpu
from jax.sharding import PartitionSpec as P

R = 8
STEPS = 4
HD = 128
GROUP = 7
ROWS = 32
BLOCK = 512
NBLK = 64
COUNT = 32
LAG = 8
CHUNK = 16
NCHUNK = NBLK // CHUNK
FLOOR = -1e30
RATE = math.log2(math.e) / math.sqrt(HD)
MESH = pl.DeviceIdType.MESH


def hops(k):
    ring = (0, 1, 2, 1)
    return k // 16 + ring[k // 4 % 4] + ring[k % 4]


PEERS = sorted(range(1, COUNT), key=hops, reverse=True)


def kernel(
    q_hbm, k_hbm, v_hbm, nk_hbm, nv_hbm, len_hbm, req_hbm, idx_hbm, out_ref,
    kb, vb, kt, wb, keep, sm, sl, sa, qrow, qbuf, qs, nk, nv, msg, part,
    clen, req, idx, prev, ksem, vsem, small, q_send, q_recv, p_send, p_recv,
):
    me = lax.axis_index("seq")

    barrier = pltpu.get_barrier_semaphore()
    for k in PEERS:
        pl.semaphore_signal(barrier, inc=1, device_id={"seq": me ^ k}, device_id_type=MESH)

    small_copies = [
        pltpu.make_async_copy(src, dst, small.at[i])
        for i, (src, dst) in enumerate(
            ((q_hbm, qrow), (req_hbm, req), (idx_hbm, idx), (len_hbm, clen), (nk_hbm, nk), (nv_hbm, nv))
        )
    ]
    for copy in small_copies:
        copy.start()

    def k_copy(i):
        rows = pl.ds(i * CHUNK, CHUNK)
        return pltpu.make_async_copy(k_hbm.at[rows], kb.at[rows], ksem.at[i])

    def v_copy(i):
        rows = pl.ds(i * CHUNK, CHUNK)
        return pltpu.make_async_copy(v_hbm.at[rows], vb.at[rows], vsem.at[i])

    for i in range(NCHUNK):
        k_copy(i).start()
    for i in range(NCHUNK):
        v_copy(i).start()

    small_copies[0].wait()
    own = qrow[...].astype(jnp.float32)
    own = jnp.concatenate(
        [own[:, g * HD : (g + 1) * HD] for g in range(GROUP)] + [jnp.zeros((1, HD), jnp.float32)],
        axis=0,
    )
    qbuf[me] = own.astype(jnp.bfloat16)
    pl.semaphore_wait(barrier, COUNT - 1)
    for k in PEERS:
        pltpu.make_async_remote_copy(
            src_ref=qbuf.at[me],
            dst_ref=qbuf.at[me],
            send_sem=q_send,
            recv_sem=q_recv,
            device_id={"seq": me ^ k},
            device_id_type=MESH,
        ).start()

    for copy in small_copies[1:]:
        copy.wait()
    sm[0] = jnp.full((ROWS, HD), FLOOR, jnp.float32)
    sl[0] = jnp.zeros((ROWS, HD), jnp.float32)
    sa[0] = jnp.zeros((ROWS, HD), jnp.float32)

    def link(b, last):
        r = req[b]
        before = last[0]
        for j in range(1, R):
            before = jnp.where(r == j, last[j], before)
        prev[b] = before
        return tuple(jnp.where(r == j, b + 1, last[j]) for j in range(R))

    last = lax.fori_loop(0, NBLK, link, tuple(jnp.int32(0) for _ in range(R)))

    lane8 = lax.broadcasted_iota(jnp.int32, (8, HD), 1)
    row8 = lax.broadcasted_iota(jnp.int32, (8, HD), 0)

    own_request = me // STEPS
    own_step = me % STEPS
    fresh_k = nk[own_request].astype(jnp.float32)
    fresh_v = nv[own_request].astype(jnp.float32)
    fresh_s = []
    for u in range(STEPS):
        s = jnp.sum(own * fresh_k[u : u + 1, :], axis=1, keepdims=True)
        fresh_s.append(jnp.where(u <= own_step, jnp.broadcast_to(s, (8, HD)), FLOOR))
    fresh_m = fresh_s[0]
    for u in range(1, STEPS):
        fresh_m = jnp.maximum(fresh_m, fresh_s[u])
    fresh_l = jnp.zeros((8, HD), jnp.float32)
    fresh_a = jnp.zeros((8, HD), jnp.float32)
    for u in range(STEPS):
        w = jnp.exp2((fresh_s[u] - fresh_m) * RATE).astype(jnp.bfloat16).astype(jnp.float32)
        fresh_l = fresh_l + w
        fresh_a = fresh_a + w * fresh_v[u : u + 1, :]

    def turn(*columns):
        picked = 0.0
        for i, column in enumerate(columns):
            picked = jnp.where(lane8 == row8 + 8 * i, column, picked)
        return jnp.sum(picked, axis=0, keepdims=True)

    fresh_m_row = turn(fresh_m)
    fresh_l_row = turn(fresh_l)

    def turn_keys(i, _):
        for u in range(4):
            kt[i * 4 + u] = kb[i * 4 + u].T
        return 0

    for i in range(NCHUNK):
        k_copy(i).wait()
        lax.fori_loop(i * CHUNK // 4, (i + 1) * CHUNK // 4, turn_keys, 0)

    for i in range(NCHUNK):
        v_copy(i).wait()

    others = qbuf.at[pl.ds(0, COUNT - 1)]
    pltpu.make_async_copy(others, others, q_recv).wait()
    for r in range(R):
        qs[r] = qbuf[r * STEPS : (r + 1) * STEPS].astype(jnp.float32).reshape(ROWS, HD).astype(jnp.bfloat16)

    lane = lax.broadcasted_iota(jnp.int32, (ROWS, HD), 1)

    def weigh(b):
        s = jnp.dot(qs[req[b]], kt[b], preferred_element_type=jnp.float32)
        limit = clen[req[b]] - idx[b] * BLOCK
        scores = []
        most = None
        for t in range(0, BLOCK, HD):
            x = jnp.where(lane < limit - t, s[:, t : t + HD], FLOOR)
            scores.append(x)
            most = x if most is None else jnp.maximum(most, x)
        before = sm[prev[b]]
        best = jnp.maximum(before, jnp.broadcast_to(jnp.max(most, axis=1, keepdims=True), (ROWS, HD)))
        sm[b + 1] = best
        shrink = jnp.exp2((before - best) * RATE)
        keep[b] = shrink
        total = None
        for t, x in zip(range(0, BLOCK, HD), scores):
            w = jnp.exp2((x - best) * RATE)
            total = w if total is None else total + w
            wb[b, :, t : t + HD] = w.astype(jnp.bfloat16)
        sl[b + 1] = sl[prev[b]] * shrink + total

    def gather_values(b):
        o = jnp.dot(wb[b], vb[b], preferred_element_type=jnp.float32)
        sa[b + 1] = sa[prev[b]] * keep[b] + o

    for b in range(NBLK + LAG):
        if b < NBLK:
            weigh(b)
        if b >= LAG:
            gather_values(b - LAG)

    for r in range(R):
        m = sm[last[r]]
        l = jnp.broadcast_to(jnp.sum(sl[last[r]], axis=1, keepdims=True), (ROWS, HD))
        for s in range(STEPS):
            rows = slice(s * 8, s * 8 + 8)
            msg[r * STEPS + s] = jnp.broadcast_to(turn(m[rows], l[rows]), (8, HD))

    for r in range(R):
        a = sa[last[r]]
        for s in range(STEPS):
            d = r * STEPS + s
            msg[d] = jnp.where(row8 == 7, msg[d], a[s * 8 : s * 8 + 8])
    for k in PEERS:
        pltpu.make_async_remote_copy(
            src_ref=msg.at[me ^ k],
            dst_ref=part.at[me],
            send_sem=p_send,
            recv_sem=p_recv,
            device_id={"seq": me ^ k},
            device_id_type=MESH,
        ).start()
    part[me] = msg[me]
    others = part.at[pl.ds(0, COUNT - 1)]
    pltpu.make_async_copy(others, others, p_recv).wait()

    m = part[:, 7, :]
    l = pltpu.roll(m, HD - 8, 1)
    best = jnp.maximum(jnp.max(m, axis=0, keepdims=True), fresh_m_row)
    w = jnp.exp2((m - best) * RATE)
    fresh_w = jnp.exp2((fresh_m_row - best) * RATE)
    total = jnp.sum(w * l, axis=0, keepdims=True) + fresh_w * fresh_l_row
    w = w / total
    fresh_w = fresh_w / total

    def spread(row):
        picked = jnp.where(lane8 == row8, jnp.broadcast_to(row, (8, HD)), 0.0)
        return jnp.sum(picked, axis=1, keepdims=True)

    out = spread(fresh_w) * fresh_a
    for i in range(COUNT):
        out = out + spread(w[i : i + 1, :]) * part[i]
    out_ref[...] = jnp.concatenate([out[g : g + 1, :] for g in range(GROUP)], axis=1).astype(jnp.bfloat16)

    sent = qbuf.at[pl.ds(0, COUNT - 1)]
    pltpu.make_async_copy(sent, sent, q_send).wait()
    sent = msg.at[pl.ds(0, COUNT - 1)]
    pltpu.make_async_copy(sent, sent, p_send).wait()


def shards(queries, keys, values, new_keys, new_values, cache_len, block_request, block_index):
    f32, bf16, i32 = jnp.float32, jnp.bfloat16, jnp.int32
    dma = pltpu.SemaphoreType.DMA
    return pl.pallas_call(
        kernel,
        out_shape=pltpu.VMEM((1, GROUP * HD), bf16),
        in_specs=[pl.BlockSpec(memory_space=pltpu.HBM)] * 8,
        out_specs=pl.BlockSpec(memory_space=pltpu.VMEM),
        scratch_shapes=[
            pltpu.VMEM((NBLK, BLOCK, HD), bf16),
            pltpu.VMEM((NBLK, BLOCK, HD), bf16),
            pltpu.VMEM((NBLK, HD, BLOCK), bf16),
            pltpu.VMEM((NBLK, ROWS, BLOCK), bf16),
            pltpu.VMEM((NBLK, ROWS, HD), f32),
            pltpu.VMEM((NBLK + 1, ROWS, HD), f32),
            pltpu.VMEM((NBLK + 1, ROWS, HD), f32),
            pltpu.VMEM((NBLK + 1, ROWS, HD), f32),
            pltpu.VMEM((1, GROUP * HD), bf16),
            pltpu.VMEM((COUNT, 8, HD), bf16),
            pltpu.VMEM((R, ROWS, HD), bf16),
            pltpu.VMEM((R, STEPS, HD), bf16),
            pltpu.VMEM((R, STEPS, HD), bf16),
            pltpu.VMEM((COUNT, 8, HD), f32),
            pltpu.VMEM((COUNT, 8, HD), f32),
            pltpu.SMEM((R,), i32),
            pltpu.SMEM((NBLK,), i32),
            pltpu.SMEM((NBLK,), i32),
            pltpu.SMEM((NBLK,), i32),
            dma((NCHUNK,)),
            dma((NCHUNK,)),
            dma((6,)),
            dma,
            dma,
            dma,
            dma,
        ],
        compiler_params=pltpu.CompilerParams(
            collective_id=0, has_side_effects=True, vmem_limit_bytes=63 * 2**20
        ),
        name="attend",
    )(queries, keys, values, new_keys, new_values, cache_len, block_request, block_index)


def solution(mesh):
    return jax.shard_map(
        shards,
        mesh=mesh,
        in_specs=(
            P("seq", "kvh"),
            P("seq", None, "kvh"),
            P("seq", None, "kvh"),
            P(None, None, "kvh"),
            P(None, None, "kvh"),
            P(),
            P("seq"),
            P("seq"),
        ),
        out_specs=P("seq", "kvh"),
        check_vma=False,
    )
```

```python
import math

import jax
import jax.numpy as jnp
from jax import lax
from jax.experimental import pallas as pl
from jax.experimental.pallas import tpu as pltpu
from jax.sharding import PartitionSpec as P

R = 8
STEPS = 4
HD = 128
GROUP = 7
ROWS = 32
BLOCK = 512
NBLK = 64
COUNT = 32
LAG = 8
CHUNK = 16
NCHUNK = NBLK // CHUNK
FLOOR = -1e30
RATE = math.log2(math.e) / math.sqrt(HD)
MESH = pl.DeviceIdType.MESH


def hops(k):
    ring = (0, 1, 2, 1)
    return k // 16 + ring[k // 4 % 4] + ring[k % 4]


def peer(me, k):
    return (me // 16 + k // 16) % 2 * 16 + (me // 4 + k // 4) % 4 * 4 + (me + k) % 4


PEERS = sorted(range(1, COUNT), key=hops, reverse=True)


def kernel(
    q_hbm, k_hbm, v_hbm, nk_hbm, nv_hbm, len_hbm, req_hbm, idx_hbm, out_ref,
    kb, vb, kt, wb, keep, sm, sl, sa, qrow, qbuf, qs, nk, nv, msg, part,
    clen, req, idx, prev, ksem, vsem, small, q_send, q_recv, p_send, p_recv,
):
    me = lax.axis_index("seq")

    barrier = pltpu.get_barrier_semaphore()
    for k in PEERS:
        pl.semaphore_signal(barrier, inc=1, device_id={"seq": peer(me, k)}, device_id_type=MESH)

    small_copies = [
        pltpu.make_async_copy(src, dst, small.at[i])
        for i, (src, dst) in enumerate(
            ((q_hbm, qrow), (req_hbm, req), (idx_hbm, idx), (len_hbm, clen), (nk_hbm, nk), (nv_hbm, nv))
        )
    ]
    for copy in small_copies:
        copy.start()

    def k_copy(i):
        rows = pl.ds(i * CHUNK, CHUNK)
        return pltpu.make_async_copy(k_hbm.at[rows], kb.at[rows], ksem.at[i])

    def v_copy(i):
        rows = pl.ds(i * CHUNK, CHUNK)
        return pltpu.make_async_copy(v_hbm.at[rows], vb.at[rows], vsem.at[i])

    for i in range(NCHUNK):
        k_copy(i).start()
    for i in range(NCHUNK):
        v_copy(i).start()

    small_copies[0].wait()
    own = qrow[...].astype(jnp.float32)
    own = jnp.concatenate(
        [own[:, g * HD : (g + 1) * HD] for g in range(GROUP)] + [jnp.zeros((1, HD), jnp.float32)],
        axis=0,
    )
    qbuf[me] = own.astype(jnp.bfloat16)
    pl.semaphore_wait(barrier, COUNT - 1)
    for k in PEERS:
        pltpu.make_async_remote_copy(
            src_ref=qbuf.at[me],
            dst_ref=qbuf.at[me],
            send_sem=q_send,
            recv_sem=q_recv,
            device_id={"seq": peer(me, k)},
            device_id_type=MESH,
        ).start()

    for copy in small_copies[1:]:
        copy.wait()
    sm[0] = jnp.full((ROWS, HD), FLOOR, jnp.float32)
    sl[0] = jnp.zeros((ROWS, HD), jnp.float32)
    sa[0] = jnp.zeros((ROWS, HD), jnp.float32)

    def link(b, last):
        r = req[b]
        before = last[0]
        for j in range(1, R):
            before = jnp.where(r == j, last[j], before)
        prev[b] = before
        return tuple(jnp.where(r == j, b + 1, last[j]) for j in range(R))

    last = lax.fori_loop(0, NBLK, link, tuple(jnp.int32(0) for _ in range(R)))

    lane8 = lax.broadcasted_iota(jnp.int32, (8, HD), 1)
    row8 = lax.broadcasted_iota(jnp.int32, (8, HD), 0)

    own_request = me // STEPS
    own_step = me % STEPS
    fresh_k = nk[own_request].astype(jnp.float32)
    fresh_v = nv[own_request].astype(jnp.float32)
    fresh_s = []
    for u in range(STEPS):
        s = jnp.sum(own * fresh_k[u : u + 1, :], axis=1, keepdims=True)
        fresh_s.append(jnp.where(u <= own_step, jnp.broadcast_to(s, (8, HD)), FLOOR))
    fresh_m = fresh_s[0]
    for u in range(1, STEPS):
        fresh_m = jnp.maximum(fresh_m, fresh_s[u])
    fresh_l = jnp.zeros((8, HD), jnp.float32)
    fresh_a = jnp.zeros((8, HD), jnp.float32)
    for u in range(STEPS):
        w = jnp.exp2((fresh_s[u] - fresh_m) * RATE).astype(jnp.bfloat16).astype(jnp.float32)
        fresh_l = fresh_l + w
        fresh_a = fresh_a + w * fresh_v[u : u + 1, :]

    def turn(*columns):
        picked = 0.0
        for i, column in enumerate(columns):
            picked = jnp.where(lane8 == row8 + 8 * i, column, picked)
        return jnp.sum(picked, axis=0, keepdims=True)

    fresh_m_row = turn(fresh_m)
    fresh_l_row = turn(fresh_l)

    def turn_keys(i, _):
        for u in range(4):
            kt[i * 4 + u] = kb[i * 4 + u].T
        return 0

    for i in range(NCHUNK):
        k_copy(i).wait()
        lax.fori_loop(i * CHUNK // 4, (i + 1) * CHUNK // 4, turn_keys, 0)

    for i in range(NCHUNK):
        v_copy(i).wait()

    others = qbuf.at[pl.ds(0, COUNT - 1)]
    pltpu.make_async_copy(others, others, q_recv).wait()
    for r in range(R):
        qs[r] = qbuf[r * STEPS : (r + 1) * STEPS].astype(jnp.float32).reshape(ROWS, HD).astype(jnp.bfloat16)

    lane = lax.broadcasted_iota(jnp.int32, (ROWS, HD), 1)

    def weigh(b):
        s = jnp.dot(qs[req[b]], kt[b], preferred_element_type=jnp.float32)
        limit = clen[req[b]] - idx[b] * BLOCK
        scores = []
        most = None
        for t in range(0, BLOCK, HD):
            x = jnp.where(lane < limit - t, s[:, t : t + HD], FLOOR)
            scores.append(x)
            most = x if most is None else jnp.maximum(most, x)
        before = sm[prev[b]]
        best = jnp.maximum(before, jnp.broadcast_to(jnp.max(most, axis=1, keepdims=True), (ROWS, HD)))
        sm[b + 1] = best
        shrink = jnp.exp2((before - best) * RATE)
        keep[b] = shrink
        total = None
        for t, x in zip(range(0, BLOCK, HD), scores):
            w = jnp.exp2((x - best) * RATE)
            total = w if total is None else total + w
            wb[b, :, t : t + HD] = w.astype(jnp.bfloat16)
        sl[b + 1] = sl[prev[b]] * shrink + total

    def gather_values(b):
        o = jnp.dot(wb[b], vb[b], preferred_element_type=jnp.float32)
        sa[b + 1] = sa[prev[b]] * keep[b] + o

    for b in range(NBLK + LAG):
        if b < NBLK:
            weigh(b)
        if b >= LAG:
            gather_values(b - LAG)

    for r in range(R):
        m = sm[last[r]]
        l = jnp.broadcast_to(jnp.sum(sl[last[r]], axis=1, keepdims=True), (ROWS, HD))
        for s in range(STEPS):
            rows = slice(s * 8, s * 8 + 8)
            msg[r * STEPS + s] = jnp.broadcast_to(turn(m[rows], l[rows]), (8, HD))

    for r in range(R):
        a = sa[last[r]]
        for s in range(STEPS):
            d = r * STEPS + s
            msg[d] = jnp.where(row8 == 7, msg[d], a[s * 8 : s * 8 + 8])
    for k in PEERS:
        pltpu.make_async_remote_copy(
            src_ref=msg.at[peer(me, k)],
            dst_ref=part.at[me],
            send_sem=p_send,
            recv_sem=p_recv,
            device_id={"seq": peer(me, k)},
            device_id_type=MESH,
        ).start()
    part[me] = msg[me]
    others = part.at[pl.ds(0, COUNT - 1)]
    pltpu.make_async_copy(others, others, p_recv).wait()

    m = part[:, 7, :]
    l = pltpu.roll(m, HD - 8, 1)
    best = jnp.maximum(jnp.max(m, axis=0, keepdims=True), fresh_m_row)
    w = jnp.exp2((m - best) * RATE)
    fresh_w = jnp.exp2((fresh_m_row - best) * RATE)
    total = jnp.sum(w * l, axis=0, keepdims=True) + fresh_w * fresh_l_row
    w = w / total
    fresh_w = fresh_w / total

    def spread(row):
        picked = jnp.where(lane8 == row8, jnp.broadcast_to(row, (8, HD)), 0.0)
        return jnp.sum(picked, axis=1, keepdims=True)

    out = spread(fresh_w) * fresh_a
    for i in range(COUNT):
        out = out + spread(w[i : i + 1, :]) * part[i]
    out_ref[...] = jnp.concatenate([out[g : g + 1, :] for g in range(GROUP)], axis=1).astype(jnp.bfloat16)

    sent = qbuf.at[pl.ds(0, COUNT - 1)]
    pltpu.make_async_copy(sent, sent, q_send).wait()
    sent = msg.at[pl.ds(0, COUNT - 1)]
    pltpu.make_async_copy(sent, sent, p_send).wait()


def shards(queries, keys, values, new_keys, new_values, cache_len, block_request, block_index):
    f32, bf16, i32 = jnp.float32, jnp.bfloat16, jnp.int32
    dma = pltpu.SemaphoreType.DMA
    return pl.pallas_call(
        kernel,
        out_shape=pltpu.VMEM((1, GROUP * HD), bf16),
        in_specs=[pl.BlockSpec(memory_space=pltpu.HBM)] * 8,
        out_specs=pl.BlockSpec(memory_space=pltpu.VMEM),
        scratch_shapes=[
            pltpu.VMEM((NBLK, BLOCK, HD), bf16),
            pltpu.VMEM((NBLK, BLOCK, HD), bf16),
            pltpu.VMEM((NBLK, HD, BLOCK), bf16),
            pltpu.VMEM((NBLK, ROWS, BLOCK), bf16),
            pltpu.VMEM((NBLK, ROWS, HD), f32),
            pltpu.VMEM((NBLK + 1, ROWS, HD), f32),
            pltpu.VMEM((NBLK + 1, ROWS, HD), f32),
            pltpu.VMEM((NBLK + 1, ROWS, HD), f32),
            pltpu.VMEM((1, GROUP * HD), bf16),
            pltpu.VMEM((COUNT, 8, HD), bf16),
            pltpu.VMEM((R, ROWS, HD), bf16),
            pltpu.VMEM((R, STEPS, HD), bf16),
            pltpu.VMEM((R, STEPS, HD), bf16),
            pltpu.VMEM((COUNT, 8, HD), f32),
            pltpu.VMEM((COUNT, 8, HD), f32),
            pltpu.SMEM((R,), i32),
            pltpu.SMEM((NBLK,), i32),
            pltpu.SMEM((NBLK,), i32),
            pltpu.SMEM((NBLK,), i32),
            dma((NCHUNK,)),
            dma((NCHUNK,)),
            dma((6,)),
            dma,
            dma,
            dma,
            dma,
        ],
        compiler_params=pltpu.CompilerParams(
            collective_id=0, has_side_effects=True, vmem_limit_bytes=63 * 2**20
        ),
        name="attend",
    )(queries, keys, values, new_keys, new_values, cache_len, block_request, block_index)


def solution(mesh):
    return jax.shard_map(
        shards,
        mesh=mesh,
        in_specs=(
            P("seq", "kvh"),
            P("seq", None, "kvh"),
            P("seq", None, "kvh"),
            P(None, None, "kvh"),
            P(None, None, "kvh"),
            P(),
            P("seq"),
            P("seq"),
        ),
        out_specs=P("seq", "kvh"),
        check_vma=False,
    )
```
